32 devices in a mesh: runs: 2 (over y), gx: 4 (over z), gy: 2 (over x), wa: 2 (over core).
Axes of the slice: x: 2, y: 2, z: 4, core: 2. Of those that a mesh axis runs over, the one named last changes fastest.
Arguments:
- slabs: float32 [6, 16, 256, 1024], P('runs', 'wa', 'gx', 'gy'), parts along dimension 0, may hold values from -6 to 6
- slab_index: int32 [6], P('runs'), parts along dimension 0, may hold values from 0 to 31
- omega_x: float32 [256, 64], P('gx'), may hold values from -0.375 to 0.375
- omega_y: float32 [1024, 64], P('gy'), may hold values from -0.1875 to 0.1875
- omega_z: float32 [512, 64], replicated, may hold values from -1.5 to 1.5
- phi_x: float32 [256, 128], P('gx'), may hold values from -0.375 to 0.375
- phi_y: float32 [1024, 128], P('gy'), may hold values from -0.1875 to 0.1875
- phi_z: float32 [512, 64], replicated, may hold values from -1.5 to 1.5
- sketch_x: float32 [512, 64], P(('runs', 'gx')), parts along dimension 0, may hold values from -6 to 6
- sketch_y: float32 [2048, 64], P(('runs', 'gy')), parts along dimension 0, may hold values from -6 to 6
- sketch_z: float32 [1024, 64], P('runs'), parts along dimension 0, may hold values from -6 to 6
- core: float32 [128, 128, 128], P(('runs', 'wa'), 'gx', 'gy'), parts along dimension 0, may hold values from -6 to 6
Outputs:
- new_sketch_x: float32 [512, 64], P(('runs', 'gx')), parts along dimension 0
- new_sketch_y: float32 [2048, 64], P(('runs', 'gy')), parts along dimension 0
- new_sketch_z: float32 [1024, 64], P('runs'), parts along dimension 0
- new_core: float32 [128, 128, 128], P(('runs', 'wa'), 'gx', 'gy'), parts along dimension 0
The draws below stay inside these ranges and needn't reach their ends.
There are 2 independent parts, one for each index of `runs`. The reference program is written for one: setup_inputs(seed, part) draws one part's arguments, and reference() takes and returns one part's arrays. A program takes and returns all parts, laid end to end along the dimension named above; an argument that names none is the same for every part. Nothing has to cross between parts.
Inputs may be any that keep to these rules, and one draw needn't show every extreme that they name: `slab_index`: steps may bring the same slab more than once.
All inputs are finite; a program needn't handle non-finite values.
Results may differ from the reference program's by a relative error of at most 0.0001.
Values sent between devices are 32-bit elements; how exact they have to be, the bound alone decides.
A program may use at most 64 MiB of HBM per device.

```python
import jax
import jax.numpy as jnp
from jax import lax

DZ = 16
NSLAB = 32
STEPS = 3
R = 64
S = 128
SZ = 64
I = 256
J = 1024
K = 512


def steps_of(own_key, dims, split, least, high):
    def one(axis_at, shards_of):
        steps = jax.random.uniform(jax.random.fold_in(jax.random.fold_in(own_key, 6), axis_at), (shards_of,), jnp.float32, least / len(split), high / len(split))
        return jnp.repeat(jnp.exp(steps), dims[axis_at] // shards_of).reshape((-1,) + (1,) * (len(dims) - axis_at - 1))

    loudness = one(*split[0])
    for cut in split[1:]:
        loudness = loudness * one(*cut)
    return loudness


def noise(key, dims, width, limit, split=(), kind=jnp.bfloat16):
    entries = jax.random.normal(key, dims, jnp.float32) * width
    if len(split) > 0:
        entries = steps_of(key, dims, split, -0.22, 0.18) * entries
    return jnp.clip(entries, min=-limit, max=limit).astype(kind)


def setup_inputs(seed: int = 0, part: int = 0) -> dict:
    streams_of = jax.random.split(jax.random.key(seed), 13)
    part_keys = jax.random.split(jax.random.fold_in(streams_of[12], part), 13)
    return {
        "slabs": noise(part_keys[0], (STEPS, DZ, I, J), 1.0, 6.0, ((1, 2), (2, 4), (3, 2)), jnp.float32),
        "slab_index": jax.random.randint(part_keys[1], (STEPS,), 0, NSLAB).astype(jnp.int32),
        "omega_x": noise(streams_of[2], (I, R), I ** -0.5, 0.375, ((0, 4),), jnp.float32),
        "omega_y": noise(streams_of[3], (J, R), J ** -0.5, 0.1875, ((0, 2),), jnp.float32),
        "omega_z": noise(streams_of[4], (K, R), DZ ** -0.5, 1.5, (), jnp.float32),
        "phi_x": noise(streams_of[5], (I, S), I ** -0.5, 0.375, ((0, 4),), jnp.float32),
        "phi_y": noise(streams_of[6], (J, S), J ** -0.5, 0.1875, ((0, 2),), jnp.float32),
        "phi_z": noise(streams_of[7], (K, SZ), DZ ** -0.5, 1.5, (), jnp.float32),
        "sketch_x": noise(part_keys[8], (I, R), 1.0, 6.0, ((0, 4),), jnp.float32),
        "sketch_y": noise(part_keys[9], (J, R), 1.0, 6.0, ((0, 2),), jnp.float32),
        "sketch_z": noise(part_keys[10], (K, R), 1.0, 6.0, (), jnp.float32),
        "core": noise(part_keys[11], (SZ, S, S), 1.0, 6.0, ((0, 2), (1, 4), (2, 2)), jnp.float32),
    }


def contract(form, left, right):
    return jnp.einsum(form, left, right, precision=lax.Precision.HIGHEST)


def reference(slabs, slab_index, omega_x, omega_y, omega_z, phi_x, phi_y, phi_z, sketch_x, sketch_y, sketch_z, core):
    for step in range(STEPS):
        field = slabs[step]
        start = (slab_index[step] * DZ).astype(jnp.int32)
        depth_omega = lax.dynamic_slice_in_dim(omega_z, start, DZ, 0)
        depth_phi = lax.dynamic_slice_in_dim(phi_z, start, DZ, 0)
        row_mix = contract("zij,jr->zir", field, omega_y)
        sketch_x = sketch_x + contract("zir,zr->ir", row_mix, depth_omega)
        plane_rows = contract("zir,ir->zr", row_mix, omega_x)
        col_mix = contract("zij,ir->zjr", field, omega_x)
        sketch_y = sketch_y + contract("zjr,zr->jr", col_mix, depth_omega)
        current = lax.dynamic_slice_in_dim(sketch_z, start, DZ, 0)
        sketch_z = lax.dynamic_update_slice_in_dim(sketch_z, current + plane_rows, start, 0)
        core_cols = contract("zij,jb->zib", field, phi_y)
        core_both = contract("zib,ia->zab", core_cols, phi_x)
        core = core + contract("zab,zc->cab", core_both, depth_phi)
    return sketch_x, sketch_y, sketch_z, core
```

```python
import functools

import jax
import jax.numpy as jnp
from jax import lax
from jax.experimental import pallas as pl
from jax.experimental.pallas import tpu as pltpu
from jax.sharding import PartitionSpec as P

DZ = 16
F32 = jnp.float32
BF16 = jnp.bfloat16
LANES = 128
NN = (((1,), (0,)), ((), ()))
NT = (((1,), (1,)), ((), ()))


def contract(form, left, right):
    return jnp.einsum(form, left, right, precision=lax.Precision.HIGHEST)


def split(value):
    high = value.astype(BF16)
    return high, (value - high.astype(F32)).astype(BF16)


def mul(left, right, dims=NN):
    return lax.dot_general(left, right, dims, preferred_element_type=F32)


def mul3(left_high, left_low, right_high, right_low, dims=NN):
    rows = left_high.shape[0]
    both = mul(jnp.concatenate([left_high, left_low], axis=0), right_high, dims)
    return both[:rows] + both[rows:] + mul(left_high, right_low, dims)


def iota(shape, dim):
    return lax.broadcasted_iota(jnp.int32, shape, dim)


def fused(
    steps, planes, rows, row_width, col_width,
    index, slabs, omega_x, omega_y, omega_z, phi_x, phi_y, phi_z, sketch_x, sketch_y, sketch_z, core,
    new_x, new_y, new_z, new_core,
    v_slabs, v_ox, v_oy, v_oz, v_px, v_py, v_pz, v_sx, v_sy, v_sz, v_core, in_sem,
    gy_out, gy_in, cols, px_in, raw_in, keep, mid_out, mid_in, end_out, end_in, total, wa_in,
    mix, own_high, own_low, far_high, far_low, y_sum, x_sum, z_sum, hot, depth,
    g1_out, g1_in, g2_out, g2_in, ga_out, ga_in, gb_out, gb_in, gc_in, g4_out, g4_in, cube,
    o_x, o_y, o_z, o_core, out_sem, send_sem, recv_sem,
):
    gx, gy, wa = lax.axis_index("gx"), lax.axis_index("gy"), lax.axis_index("wa")
    pair = gx + 1 - 2 * lax.rem(gx, 2)
    across = 3 - gx
    inner = jnp.logical_or(gx == 1, gx == 2)
    outer = jnp.logical_not(inner)
    group = LANES // row_width
    quads = planes // group
    full = v_px.shape[1]
    rank = v_oy.shape[0]
    half = rank // 2
    n_sems = [0]

    def local(src, dst, sem):
        return pltpu.make_async_copy(src, dst, sem)

    sources = (phi_y, omega_y, omega_z, omega_x, phi_x, phi_z, sketch_x, sketch_y, sketch_z, core)
    places = (v_py, v_oy, v_oz, v_ox, v_px, v_pz, v_sx, v_sy, v_sz, v_core)
    loads = [local(s, d, in_sem.at[k]) for k, (s, d) in enumerate(zip(sources, places))]
    fields = [local(slabs.at[t], v_slabs.at[t], in_sem.at[len(loads) + t]) for t in range(steps)]
    for copy in loads[:2] + fields[:1] + loads[2:6] + fields[1:] + loads[6:]:
        copy.start()

    barrier = pltpu.get_barrier_semaphore()
    for where in ({"wa": 1 - wa}, {"gy": 1 - gy}, {"gx": pair}):
        pl.semaphore_signal(barrier, inc=1, device_id=where, device_id_type=pl.DeviceIdType.MESH)

    @pl.when(inner)
    def _():
        pl.semaphore_signal(barrier, inc=1, device_id={"gx": across}, device_id_type=pl.DeviceIdType.MESH)

    def remote(src, dst, where):
        k = n_sems[0]
        n_sems[0] += 1
        return pltpu.make_async_remote_copy(
            src_ref=src, dst_ref=dst, send_sem=send_sem.at[k], recv_sem=recv_sem.at[k],
            device_id=where, device_id_type=pl.DeviceIdType.MESH,
        )

    to_gy = [remote(gy_out.at[t], gy_in.at[t], {"gy": 1 - gy}) for t in range(steps)]
    to_px = remote(v_px, px_in, {"gx": pair})
    to_raw = [remote(cols.at[t], raw_in.at[t], {"gx": pair}) for t in range(steps)]
    to_mid = [remote(mid_out.at[t], mid_in.at[t], {"gx": across}) for t in range(steps)]
    to_end = [remote(end_out.at[t], end_in.at[t], {"gx": pair}) for t in range(steps)]
    to_wa = [remote(total.at[t], wa_in.at[t], {"wa": 1 - wa}) for t in range(steps)]
    to_g1 = remote(g1_out, g1_in, {"wa": 1 - wa})
    to_g2 = remote(g2_out, g2_in, {"gy": 1 - gy})
    to_ga = remote(ga_out, ga_in, {"gx": pair})
    to_gb = remote(gb_out, gb_in, {"gx": across})
    to_gc = remote(g4_out, gc_in, {"gx": pair})
    to_g4 = remote(g4_out, g4_in, {"wa": 1 - wa})

    loads[0].wait()
    loads[1].wait()
    for k, part in enumerate(split(jnp.concatenate([v_py[...].T, v_oy[...]], axis=0))):
        mix[k] = part

    loads[2].wait()
    loads[3].wait()
    loads[4].wait()
    loads[5].wait()
    depth_count = steps * planes

    def rows_of(offsets):
        lane = iota((v_oz.shape[1], LANES), 1)
        wanted = jnp.full(lane.shape, -1, jnp.int32)
        for k, offset in enumerate(offsets):
            for t in range(steps):
                first = k * depth_count + t * planes
                inside = jnp.logical_and(lane >= first, lane < first + planes)
                wanted = jnp.where(inside, lane - first + (index[t] * DZ + offset), wanted)
        return (iota(lane.shape, 0) == wanted).astype(BF16)

    here, there = wa * planes, (1 - wa) * planes
    hot[0] = rows_of((here, there))
    hot[1] = rows_of((there,))
    oz_high, oz_low = (mul(part, hot[0]).astype(BF16) for part in split(v_oz[...]))
    for k, part in enumerate(split(v_pz[...])):
        depth[k] = mul(part, hot[0])
    ox_t = v_ox[...].T
    ox_tiles = jnp.concatenate([ox_t] * planes, axis=1)
    def compute(t):
        fields[t].wait()
        x_high, x_low = split(v_slabs[t])
        mixed = mul3(mix[0], mix[1], x_high, x_low, NT)
        for k in range(2):
            @pl.when(gy == k)
            def _():
                cols[t] = mixed[k * col_width:(k + 1) * col_width]
                gy_out[t] = mixed[(1 - k) * col_width:(2 - k) * col_width]
        row_mix = mixed[full:]
        shape = (LANES, planes * rows)
        spread = (iota(shape, 0) == t * planes + iota(shape, 1) // rows).astype(BF16)
        weight = mul(oz_high, spread) + mul(oz_low, spread)
        w_high, w_low = split(weight * ox_tiles)
        y_part = mul3(w_high, w_low, x_high, x_low)
        weighted = row_mix * weight
        x_part = functools.reduce(
            jnp.add, [weighted[:, k:k + LANES] for k in range(0, planes * rows, LANES)]
        )
        m_high, m_low = split(row_mix * ox_tiles)
        z_part = mul(m_high, spread, NT) + mul(m_low, spread, NT)
        if t == 0:
            y_sum[...] = y_part
            x_sum[...] = x_part
            z_sum[...] = z_part
        else:
            y_sum[...] += y_part
            x_sum[...] += x_part
            z_sum[...] += z_part

    def blocks_of(phi, high_ref, low_ref):
        phi_high, phi_low = split(phi)
        k, l = iota((full, LANES), 0), iota((full, LANES), 1)
        owners = (gx, pair, across, across + 1 - 2 * lax.rem(across, 2))
        same = iota((group * rows, LANES), 0) // rows == iota((group * rows, LANES), 1) // row_width
        for o, owner in enumerate(owners):
            chosen = (k == owner * row_width + lax.rem(l, row_width)).astype(BF16)
            for part, ref in ((phi_high, high_ref), (phi_low, low_ref)):
                tiled = jnp.concatenate([mul(part, chosen)] * group, axis=0)
                ref[:, o * LANES:(o + 1) * LANES] = jnp.where(same, tiled, 0.0).astype(BF16)

    def apply_x(value, high_ref, low_ref):
        stacked = jnp.concatenate(
            [value[:, q * group * rows:(q + 1) * group * rows] for q in range(quads)], axis=0
        )
        high, low = split(stacked)
        return mul3(high, low, high_ref[...], low_ref[...])

    compute(0)

    @pl.when(inner)
    def _():
        pl.semaphore_wait(barrier, 4)

    @pl.when(outer)
    def _():
        pl.semaphore_wait(barrier, 3)

    to_gy[0].start()

    @pl.when(outer)
    def _():
        to_px.start()

    for t in range(1, steps):
        compute(t)
        to_gy[t].start()

    for k in range(2):
        @pl.when(wa == k)
        def _():
            g1_out[0:half, :] = y_sum[(1 - k) * half:(2 - k) * half, :]
    fold = rank // 4
    for k in range(4):
        g1_out[half:half + fold, k * LANES:(k + 1) * LANES] = x_sum[k * fold:(k + 1) * fold, :]
    to_g1.start()

    @pl.when(inner)
    def _():
        blocks_of(v_px[...], own_high, own_low)
        to_px.wait_recv()
        blocks_of(px_in[...], far_high, far_low)

    def stage_b(t):
        to_gy[t].wait_recv()
        summed = cols[t] + gy_in[t]

        cols[t] = summed

        @pl.when(outer)
        def _():
            to_raw[t].start()

        @pl.when(inner)
        def _():
            keep[t] = apply_x(cols[t], own_high, own_low)

    def stage_c(t):
        @pl.when(inner)
        def _():
            to_raw[t].wait_recv()
            both = keep[t] + apply_x(raw_in[t], far_high, far_low)
            keep[t] = both
            mid_out[t] = both[:, 2 * LANES:]
            to_mid[t].start()

    def stage_d(t):
        @pl.when(inner)
        def _():
            to_mid[t].wait_recv()
            end_out[t] = keep[t, :, LANES:2 * LANES] + mid_in[t, :, LANES:]
            to_end[t].start()
            total[t] = keep[t, :, :LANES] + mid_in[t, :, :LANES]

    def stage_e(t):
        @pl.when(outer)
        def _():
            to_end[t].wait_recv()
            total[t] = end_in[t]
        to_wa[t].start()
        turn(0, t, total)

    def turn(which, t, ref):
        for q in range(quads):
            first = (which * steps + t) * planes * row_width + q * LANES
            cube[first:first + LANES, :] = ref[t, q * col_width:(q + 1) * col_width, :].T

    def stage_f(t):
        to_wa[t].wait_recv()
        turn(1, t, wa_in)

    def g1():
        to_g1.wait_recv()
        for k in range(2):
            @pl.when(wa == k)
            def _():
                ga_out[0:half, :] = y_sum[k * half:(k + 1) * half, :] + g1_in[0:half, :]
        g2_out[0:fold, :] = g1_out[half:half + fold, :] + g1_in[half:half + fold, :]
        for k in range(4):
            g2_out[fold:, k * LANES:(k + 1) * LANES] = z_sum[k * fold:(k + 1) * fold, :]
        to_g2.start()

    def g2():
        to_g2.wait_recv()
        ga_out[half:, :] = g2_out[fold:, :] + g2_in[fold:, :]

        @pl.when(outer)
        def _():
            to_ga.start()

        x_all = g2_out[0:fold, :] + g2_in[0:fold, :]
        x_all = jnp.concatenate([x_all[:, k * LANES:(k + 1) * LANES] for k in range(4)], axis=0)
        loads[6].wait()
        o_x[...] = v_sx[...] + (x_all[:, :rows] + x_all[:, rows:]).T
        local(o_x, new_x, out_sem.at[0]).start()

    def g3():
        @pl.when(inner)
        def _():
            to_ga.wait_recv()
            gb_out[...] = ga_out[...] + ga_in[...]
            to_gb.start()

    def g4():
        @pl.when(inner)
        def _():
            to_gb.wait_recv()
            g4_out[...] = gb_out[...] + gb_in[...]
            to_gc.start()

    def g5():
        @pl.when(outer)
        def _():
            to_gc.wait_recv()
            g4_out[...] = gc_in[...]
        to_g4.start()

    def g6():
        to_g4.wait_recv()
        loads[7].wait()
        loads[8].wait()
        for k in range(2):
            @pl.when(wa == k)
            def _():
                lower, upper = (g4_out, g4_in) if k == 0 else (g4_in, g4_out)
                o_y[0:half, :] = v_sy[0:half, :] + lower[0:half, :]
                o_y[half:, :] = v_sy[half:, :] + upper[0:half, :]
        value = v_sz[...]
        for ref, places in ((g4_out, hot[0]), (g4_in, hot[1])):
            added = [ref[half:, k * LANES:(k + 1) * LANES] for k in range(4)]
            for part in split(jnp.concatenate(added, axis=0)):
                value = value + mul(part, places, NT)
        o_z[...] = value
        local(o_y, new_y, out_sem.at[1]).start()
        local(o_z, new_z, out_sem.at[2]).start()

    stage_b(0)
    g1()
    stage_b(1)
    stage_c(0)
    g2()
    stage_b(2)
    stage_c(1)
    stage_d(0)
    g3()
    stage_c(2)
    stage_e(0)
    stage_d(1)
    g4()
    stage_e(1)
    g5()
    stage_f(0)
    stage_f(1)
    stage_d(2)
    g6()
    stage_e(2)
    stage_f(2)

    loads[9].wait()
    owned = v_pz.shape[0] // 2
    count = 2 * depth_count
    spot = pl.ds(pl.multiple_of(wa * owned, owned), owned)
    p_high, p_low = (depth[k, spot, :][:, :count].astype(BF16) for k in range(2))
    for a in range(row_width):
        high, low = split(cube[pl.ds(a, count, stride=row_width), :])
        spot = pl.ds(a, owned, stride=row_width)
        o_core[spot, :] = v_core[spot, :] + mul3(p_high, p_low, high, low)
    local(o_core, new_core, out_sem.at[3]).start()

    for copy in to_gy + to_wa + [to_g1, to_g2, to_g4]:
        copy.wait_send()

    @pl.when(outer)
    def _():
        for copy in to_raw + [to_px, to_ga]:
            copy.wait_send()

    @pl.when(inner)
    def _():
        for copy in to_mid + to_end + [to_gb, to_gc]:
            copy.wait_send()

    for k, (src, dst) in enumerate(((o_x, new_x), (o_y, new_y), (o_z, new_z), (o_core, new_core))):
        local(src, dst, out_sem.at[k]).wait()


def one_kernel(
    slabs, slab_index, omega_x, omega_y, omega_z, phi_x, phi_y, phi_z, sketch_x, sketch_y, sketch_z, core
):
    steps, planes, rows, width = slabs.shape
    rank, full = omega_x.shape[1], phi_x.shape[1]
    row_width, col_width = core.shape[1], core.shape[2]
    group = LANES // row_width
    quads = planes // group
    flat = planes * rows
    half, fold = rank // 2, rank // 4
    line = half + fold
    vmem = lambda shape, kind=F32: pltpu.VMEM(shape, kind)
    like = lambda value: vmem(value.shape)
    flat_core = core.reshape(-1, col_width)
    operands = (
        slabs.reshape(steps, flat, width), omega_x, omega_y.T, omega_z.T, phi_x, phi_y, phi_z.T,
        sketch_x, sketch_y.T, sketch_z.T, flat_core,
    )
    scratch = [like(value) for value in operands]
    scratch += [
        pltpu.SemaphoreType.DMA((10 + steps,)),
        vmem((steps, col_width, flat)), vmem((steps, col_width, flat)), vmem((steps, col_width, flat)),
        vmem((rows, full)), vmem((steps, col_width, flat)),
        vmem((steps, quads * col_width, 4 * LANES)),
        vmem((steps, quads * col_width, 2 * LANES)), vmem((steps, quads * col_width, 2 * LANES)),
        vmem((steps, quads * col_width, LANES)), vmem((steps, quads * col_width, LANES)),
        vmem((steps, quads * col_width, LANES)), vmem((steps, quads * col_width, LANES)),
        vmem((2, full + rank, width), BF16),
        vmem((group * rows, 4 * LANES), BF16), vmem((group * rows, 4 * LANES), BF16),
        vmem((group * rows, 4 * LANES), BF16), vmem((group * rows, 4 * LANES), BF16),
        vmem((rank, width)), vmem((rank, LANES)), vmem((rank, LANES)),
        vmem((2, omega_z.shape[0], LANES), BF16), vmem((2, phi_z.shape[1], LANES)),
        vmem((half + fold, width)), vmem((half + fold, width)),
        vmem((2 * fold, width)), vmem((2 * fold, width)),
        vmem((line, width)), vmem((line, width)), vmem((line, width)), vmem((line, width)),
        vmem((line, width)), vmem((line, width)), vmem((line, width)),
        vmem((2 * steps * planes * row_width, col_width)),
        *(like(value) for value in operands[-4:]),
        pltpu.SemaphoreType.DMA((4,)),
        pltpu.SemaphoreType.DMA((5 * steps + 7,)),
        pltpu.SemaphoreType.DMA((5 * steps + 7,)),
    ]
    outs = [jax.ShapeDtypeStruct(v.shape, F32) for v in operands[-4:]]
    new_x, new_y, new_z, new_core = pl.pallas_call(
        functools.partial(fused, steps, planes, rows, row_width, col_width),
        out_shape=outs,
        in_specs=[pl.BlockSpec(memory_space=pltpu.SMEM)] + [pl.BlockSpec(memory_space=pl.ANY)] * len(operands),
        out_specs=[pl.BlockSpec(memory_space=pl.ANY)] * 4,
        scratch_shapes=scratch,
        compiler_params=pltpu.CompilerParams(
            collective_id=0, has_side_effects=True, vmem_limit_bytes=48 * 2 ** 20
        ),
    )(slab_index, *operands)
    return new_x, new_y.T, new_z.T, new_core.reshape(core.shape)


def by_collectives(
    slabs, slab_index, omega_x, omega_y, omega_z, phi_x, phi_y, phi_z, sketch_x, sketch_y, sketch_z, core
):
    planes = slabs.shape[1]
    x_parts = lax.axis_size("gx")
    y_parts = lax.axis_size("gy")
    full_size = phi_x.shape[1]
    row_width = full_size // x_parts
    col_width = full_size // y_parts
    for step in range(slabs.shape[0]):
        field = slabs[step]
        first = slab_index[step] * DZ
        start = first + lax.axis_index("wa") * planes
        depth_omega = lax.dynamic_slice_in_dim(omega_z, start, planes, 0)
        depth_phi = lax.dynamic_slice_in_dim(phi_z, start, planes, 0)
        row_mix = contract("zij,jr->zir", field, omega_y)
        rows_part = contract("zir,zr->ir", row_mix, depth_omega)
        plane_part = contract("zir,ir->zr", row_mix, omega_x)
        col_mix = contract("zij,ir->zjr", field, omega_x)
        cols_part = contract("zjr,zr->jr", col_mix, depth_omega)
        core_cols = contract("zij,jb->zib", field, phi_y)
        sketch_x = sketch_x + lax.psum(rows_part, ("gy", "wa"))
        sketch_y = sketch_y + lax.psum(cols_part, ("gx", "wa"))
        plane_total = lax.psum(plane_part, ("gx", "gy"))
        slab_rows = lax.all_gather(plane_total, "wa", axis=0, tiled=True)
        current = lax.dynamic_slice_in_dim(sketch_z, first, DZ, 0)
        sketch_z = lax.dynamic_update_slice_in_dim(sketch_z, current + slab_rows, first, 0)
        core_both = contract("zib,ia->zab", core_cols, phi_x)
        blocks = core_both.reshape(planes, x_parts, row_width, y_parts, col_width)
        blocks = blocks.transpose(1, 3, 0, 2, 4).reshape(
            x_parts * y_parts * planes, row_width, col_width
        )
        owned = lax.psum_scatter(blocks, ("gx", "gy"), scatter_dimension=0, tiled=True)
        depth_term = contract("zab,zc->cab", owned, depth_phi)
        core = core + lax.psum_scatter(depth_term, "wa", scatter_dimension=0, tiled=True)
    return (sketch_x, sketch_y, sketch_z, core)


def solution(mesh):
    shape = dict(mesh.shape)
    in_kernel = (shape["gx"], shape["gy"], shape["wa"]) == (4, 2, 2)
    placed = (
        P("runs", "wa", "gx", "gy"),
        P("runs"),
        P("gx", None),
        P("gy", None),
        P(),
        P("gx", None),
        P("gy", None),
        P(),
        P(("runs", "gx"), None),
        P(("runs", "gy"), None),
        P("runs", None),
        P(("runs", "wa"), "gx", "gy"),
    )
    return jax.shard_map(
        one_kernel if in_kernel else by_collectives,
        mesh=mesh,
        in_specs=placed,
        out_specs=(
            P(("runs", "gx"), None),
            P(("runs", "gy"), None),
            P("runs", None),
            P(("runs", "wa"), "gx", "gy"),
        ),
        check_vma=False,
    )
```

```python
import functools

import jax
import jax.numpy as jnp
from jax import lax
from jax.experimental import pallas as pl
from jax.experimental.pallas import tpu as pltpu
from jax.sharding import PartitionSpec as P

DZ = 16
F32 = jnp.float32
BF16 = jnp.bfloat16
LANES = 128
NN = (((1,), (0,)), ((), ()))
NT = (((1,), (1,)), ((), ()))


def contract(form, left, right):
    return jnp.einsum(form, left, right, precision=lax.Precision.HIGHEST)


def split(value):
    high = value.astype(BF16)
    return high, (value - high.astype(F32)).astype(BF16)


def mul(left, right, dims=NN):
    return lax.dot_general(left, right, dims, preferred_element_type=F32)


def mul3(left_high, left_low, right_high, right_low, dims=NN):
    rows = left_high.shape[0]
    both = mul(jnp.concatenate([left_high, left_low], axis=0), right_high, dims)
    return both[:rows] + both[rows:] + mul(left_high, right_low, dims)


def iota(shape, dim):
    return lax.broadcasted_iota(jnp.int32, shape, dim)


def fused(
    steps, planes, rows, row_width, col_width,
    steps_at, slabs, omega_x, omega_y, omega_z, phi_x, phi_y, phi_z, sketch_x, sketch_y, sketch_z, core,
    o_x, o_y, o_z, o_core,
    index, v_slabs, v_ox, v_oy, v_oz, v_px, v_py, v_pz, v_sx, v_sy, v_sz, v_core, in_sem,
    gy_out, gy_in, cols, px_in, raw_in, keep, mid_in, near_in, far_in, total, wa_in,
    mix, parts, row_mix, own_high, own_low, far_high, far_low, y_sum, x_sum, z_sum, hot, depth,
    y_in, xz_out, xz_in, x_out, x_in, rs_out, rs_in, ag_out, ag_all, ag_in, cube,
    send_sem, recv_sem,
):
    gx, gy, wa = lax.axis_index("gx"), lax.axis_index("gy"), lax.axis_index("wa")
    pair = gx + 1 - 2 * lax.rem(gx, 2)
    across = 3 - gx
    beyond = 3 - pair
    inner = jnp.logical_or(gx == 1, gx == 2)
    outer = jnp.logical_not(inner)
    group = LANES // row_width
    quads = planes // group
    chunks = steps * quads
    size = group * rows
    flat = planes * rows
    full = v_px.shape[1]
    rank = v_oy.shape[0]
    half, fold = rank // 2, rank // 4
    n_sems = [0]

    def local(src, dst, sem):
        return pltpu.make_async_copy(src, dst, sem)

    sources = (phi_y, omega_y, omega_z, omega_x, phi_x, phi_z, sketch_x, sketch_y, sketch_z, core)
    places = (v_py, v_oy, v_oz, v_ox, v_px, v_pz, v_sx, v_sy, v_sz, v_core)
    loads = [local(s, d, in_sem.at[k]) for k, (s, d) in enumerate(zip(sources, places))]
    index_load = local(steps_at, index, in_sem.at[len(loads)])
    fields = []
    for c in range(chunks):
        part = (c // quads, pl.ds(c % quads * size, size))
        fields.append(local(slabs.at[part], v_slabs.at[part], in_sem.at[len(loads) + 1 + c]))
    for copy in loads[:2] + fields[:2] + [index_load] + loads[2:6] + fields[2:] + loads[6:]:
        copy.start()

    barrier = pltpu.get_barrier_semaphore()
    peers = [{"wa": 1 - wa}, {"gy": 1 - gy}, {"gx": pair}, {"gx": across}, {"gx": beyond}]
    for where in peers:
        pl.semaphore_signal(barrier, inc=1, device_id=where, device_id_type=pl.DeviceIdType.MESH)

    def remote(src, dst, where):
        k = n_sems[0]
        n_sems[0] += 1
        return pltpu.make_async_remote_copy(
            src_ref=src, dst_ref=dst, send_sem=send_sem.at[k], recv_sem=recv_sem.at[k],
            device_id=where, device_id_type=pl.DeviceIdType.MESH,
        )

    every = range(chunks)

    def block(c, k):
        return keep.at[c, :, pl.ds(k * LANES, LANES)]

    to_gy = [remote(gy_out.at[c], gy_in.at[c], {"gy": 1 - gy}) for c in every]
    to_px = remote(v_px, px_in, {"gx": pair})
    to_raw = [remote(cols.at[c], raw_in.at[c], {"gx": pair}) for c in every]
    to_near = [remote(block(c, 1), near_in.at[c], {"gx": pair}) for c in every]
    to_mid = [remote(block(c, 2), mid_in.at[c], {"gx": across}) for c in every]
    to_far = [remote(block(c, 3), far_in.at[c], {"gx": beyond}) for c in every]
    to_wa = [remote(total.at[c], wa_in.at[c], {"wa": 1 - wa}) for c in every]
    y_other = pl.ds(pl.multiple_of((1 - wa) * half, half), half)
    y_own = pl.ds(pl.multiple_of(wa * half, half), half)
    to_y = remote(y_sum.at[y_other], y_in, {"wa": 1 - wa})
    to_xz = remote(xz_out, xz_in, {"gy": 1 - gy})
    to_x = remote(x_out, x_in, {"wa": 1 - wa})
    others = (pair, across, beyond)
    to_rs = [remote(rs_out.at[o], rs_in.at[k], {"gx": o}) for k, o in enumerate(others)]
    to_ag = [remote(ag_out, ag_all.at[gx], {"gx": o}) for o in others]
    to_all = remote(ag_all, ag_in, {"wa": 1 - wa})

    loads[0].wait()
    loads[1].wait()
    for k, part in enumerate(split(jnp.concatenate([v_py[...].T, v_oy[...]], axis=0))):
        mix[k] = part

    def stage_a(c):
        fields[c].wait()
        part = (c // quads, pl.ds(c % quads * size, size))
        x_high, x_low = split(v_slabs[part])
        parts[0, c * size:(c + 1) * size, :] = x_high
        parts[1, c * size:(c + 1) * size, :] = x_low
        mixed = mul3(mix[0], mix[1], x_high, x_low, NT)
        for k in range(2):
            @pl.when(gy == k)
            def _():
                cols[c] = mixed[k * col_width:(k + 1) * col_width]
                gy_out[c] = mixed[(1 - k) * col_width:(2 - k) * col_width]
        row_mix[:, c * size:(c + 1) * size] = mixed[full:]
        if c == 0:
            pl.semaphore_wait(barrier, len(peers))

            @pl.when(outer)
            def _():
                loads[4].wait()
                to_px.start()
        to_gy[c].start()

    depth_count = steps * planes

    def rows_of(offsets):
        lane = iota((v_oz.shape[1], LANES), 1)
        wanted = jnp.full(lane.shape, -1, jnp.int32)
        for k, offset in enumerate(offsets):
            for t in range(steps):
                first = k * depth_count + t * planes
                inside = jnp.logical_and(lane >= first, lane < first + planes)
                wanted = jnp.where(inside, lane - first + (index[t] * DZ + offset), wanted)
        return (iota(lane.shape, 0) == wanted).astype(BF16)

    def sketches(t, oz_high, oz_low, ox_tiles):
        shape = (LANES, flat)
        spread = (iota(shape, 0) == t * planes + iota(shape, 1) // rows).astype(BF16)
        weight = mul(oz_high, spread) + mul(oz_low, spread)
        w_high, w_low = split(weight * ox_tiles)
        here = pl.ds(t * flat, flat)
        y_part = mul3(w_high, w_low, parts[0, here, :], parts[1, here, :])
        mixed = row_mix[:, here]
        weighted = mixed * weight
        x_part = functools.reduce(jnp.add, [weighted[:, k:k + LANES] for k in range(0, flat, LANES)])
        m_high, m_low = split(mixed * ox_tiles)
        z_part = mul(m_high, spread, NT) + mul(m_low, spread, NT)
        for ref, part in ((y_sum, y_part), (x_sum, x_part), (z_sum, z_part)):
            ref[...] = part if t == 0 else ref[...] + part

    def blocks_of(phi, high_ref, low_ref):
        phi_high, phi_low = split(phi)
        k, l = iota((full, LANES), 0), iota((full, LANES), 1)
        same = iota((size, LANES), 0) // rows == iota((size, LANES), 1) // row_width
        for o, owner in enumerate((gx, pair, across, beyond)):
            chosen = (k == owner * row_width + lax.rem(l, row_width)).astype(BF16)
            for part, ref in ((phi_high, high_ref), (phi_low, low_ref)):
                tiled = jnp.concatenate([mul(part, chosen)] * group, axis=0)
                ref[:, o * LANES:(o + 1) * LANES] = jnp.where(same, tiled, 0.0).astype(BF16)

    def stage_b(c):
        to_gy[c].wait_recv()
        cols[c] = cols[c] + gy_in[c]

        @pl.when(outer)
        def _():
            to_raw[c].start()

        @pl.when(inner)
        def _():
            high, low = split(cols[c])
            keep[c] = mul3(high, low, own_high[...], own_low[...])

    def stage_c(c):
        @pl.when(inner)
        def _():
            to_raw[c].wait_recv()
            high, low = split(raw_in[c])
            keep[c] = keep[c] + mul3(high, low, far_high[...], far_low[...])
            to_far[c].start()
            to_mid[c].start()
            to_near[c].start()

    def stage_d(c):
        @pl.when(inner)
        def _():
            to_mid[c].wait_recv()
            total[c] = keep[c, :, :LANES] + mid_in[c]

        @pl.when(outer)
        def _():
            to_near[c].wait_recv()
            to_far[c].wait_recv()
            total[c] = near_in[c] + far_in[c]

        to_wa[c].start()
        turn(0, c, total)

    def turn(which, c, ref):
        first = (which * chunks + c) * LANES
        cube[first:first + LANES, :] = ref[c].T

    def stage_f(c):
        to_wa[c].wait_recv()
        turn(1, c, wa_in)

    def sums_1():
        xz_out[:rank, :] = x_sum[...]
        xz_out[rank:, :] = z_sum[...]
        to_xz.start()
        to_y.start()

    def sums_2():
        to_y.wait_recv()
        to_xz.wait_recv()
        y_half = y_sum[y_own, :] + y_in[...]
        both = xz_out[...] + xz_in[...]
        for k in range(4):
            rs_out[k, :half, :] = y_half[:, k * LANES:(k + 1) * LANES]
            rs_out[k, half:, :] = both[rank + k * fold:rank + (k + 1) * fold]
        for copy in to_rs:
            copy.start()
        x_out[...] = both[:rank]
        to_x.start()

    def sums_3():
        for copy in to_rs:
            copy.wait_recv()
        summed = rs_out[gx] + rs_in[0] + rs_in[1] + rs_in[2]
        ag_out[...] = summed
        for copy in to_ag:
            copy.start()
        ag_all[gx] = summed

    def sums_4():
        for copy in to_ag:
            copy.wait_recv()
        to_all.start()
        to_x.wait_recv()
        x_all = x_out[...] + x_in[...]
        loads[6].wait()
        o_x[...] = v_sx[...] + (x_all[:, :rows] + x_all[:, rows:]).T

    def sums_5():
        to_all.wait_recv()
        loads[7].wait()
        loads[8].wait()
        for k in range(4):
            lanes = slice(k * LANES, (k + 1) * LANES)
            o_y[y_own, lanes] = v_sy[y_own, lanes] + ag_all[k, :half, :]
            o_y[y_other, lanes] = v_sy[y_other, lanes] + ag_in[k, :half, :]
        value = v_sz[...]
        for ref, places in ((ag_all, hot[0]), (ag_in, hot[1])):
            for part in split(jnp.concatenate([ref[k, half:, :] for k in range(4)], axis=0)):
                value = value + mul(part, places, NT)
        o_z[...] = value

    stage_a(0)
    stage_a(1)
    index_load.wait()
    for k in (2, 3, 5):
        loads[k].wait()
    hot[0] = rows_of((wa * planes, (1 - wa) * planes))
    hot[1] = rows_of(((1 - wa) * planes,))
    oz_high, oz_low = (mul(part, hot[0]).astype(BF16) for part in split(v_oz[...]))
    ox_tiles = jnp.concatenate([v_ox[...].T] * planes, axis=1)
    for c in range(2, chunks):
        stage_a(c)

    @pl.when(inner)
    def _():
        loads[4].wait()
        blocks_of(v_px[...], own_high, own_low)
        to_px.wait_recv()
        blocks_of(px_in[...], far_high, far_low)

    for t in range(steps):
        stage_b(t)
        sketches(t, oz_high, oz_low, ox_tiles)
    sums_1()
    for k, part in enumerate(split(v_pz[...])):
        depth[k] = mul(part, hot[0])
    stage_c(0)
    stage_c(1)
    extra = [sums_2, sums_3, sums_4, sums_5]
    for c in range(steps, chunks + 4):
        if c < chunks:
            stage_b(c)
        if c - 1 < chunks:
            stage_c(c - 1)
        if extra:
            extra.pop(0)()
        if 0 <= c - 3 < chunks:
            stage_d(c - 3)
        if 0 <= c - 4 < chunks:
            stage_f(c - 4)
    for action in extra:
        action()

    loads[9].wait()
    owned = v_pz.shape[0] // 2
    count = 2 * depth_count
    spot = pl.ds(pl.multiple_of(wa * owned, owned), owned)
    p_high, p_low = (depth[k, spot, :][:, :count].astype(BF16) for k in range(2))
    for a in range(row_width):
        high, low = split(cube[pl.ds(a, count, stride=row_width), :])
        spot = pl.ds(a, owned, stride=row_width)
        o_core[spot, :] = v_core[spot, :] + mul3(p_high, p_low, high, low)

    for copy in to_gy + to_wa + [to_y, to_xz, to_x, to_all] + to_rs + to_ag:
        copy.wait_send()

    @pl.when(outer)
    def _():
        for copy in to_raw + [to_px]:
            copy.wait_send()

    @pl.when(inner)
    def _():
        for copy in to_near + to_mid + to_far:
            copy.wait_send()


def hand_over(*refs):
    for source, place in zip(refs[:4], refs[4:]):
        place[...] = source[...]


def one_kernel(
    slabs, slab_index, omega_x, omega_y, omega_z, phi_x, phi_y, phi_z, sketch_x, sketch_y, sketch_z, core
):
    steps, planes, rows, width = slabs.shape
    rank, full = omega_x.shape[1], phi_x.shape[1]
    row_width, col_width = core.shape[1], core.shape[2]
    group = LANES // row_width
    chunks = steps * planes // group
    size = group * rows
    half, fold = rank // 2, rank // 4
    vmem = lambda shape, kind=F32: pltpu.VMEM(shape, kind)
    like = lambda value: vmem(value.shape)
    flat_core = core.reshape(-1, col_width)
    operands = (
        slabs.reshape(steps, planes * rows, width), omega_x, omega_y.T, omega_z.T, phi_x, phi_y, phi_z.T,
        sketch_x, sketch_y.T, sketch_z.T, flat_core,
    )
    scratch = [pltpu.SMEM(slab_index.shape, jnp.int32)] + [like(value) for value in operands]
    scratch += [
        pltpu.SemaphoreType.DMA((11 + chunks,)),
        *(vmem((chunks, col_width, size)) for _ in range(3)),
        vmem((rows, full)), vmem((chunks, col_width, size)),
        vmem((chunks, col_width, 4 * LANES)),
        *(vmem((chunks, col_width, LANES)) for _ in range(5)),
        vmem((2, full + rank, width), BF16), vmem((2, chunks * size, width), BF16), vmem((rank, chunks * size)),
        *(vmem((size, 4 * LANES), BF16) for _ in range(4)),
        vmem((rank, width)), vmem((rank, LANES)), vmem((rank, LANES)),
        vmem((2, omega_z.shape[0], LANES), BF16), vmem((2, phi_z.shape[1], LANES)),
        vmem((half, width)), vmem((2 * rank, LANES)), vmem((2 * rank, LANES)),
        vmem((rank, LANES)), vmem((rank, LANES)),
        vmem((4, half + fold, LANES)), vmem((3, half + fold, LANES)), vmem((half + fold, LANES)),
        vmem((4, half + fold, LANES)), vmem((4, half + fold, LANES)),
        vmem((2 * steps * planes * row_width, col_width)),
        pltpu.SemaphoreType.DMA((7 * chunks + 11,)),
        pltpu.SemaphoreType.DMA((7 * chunks + 11,)),
    ]
    outs = [jax.ShapeDtypeStruct(v.shape, F32) for v in operands[-4:]]
    results = pl.pallas_call(
        functools.partial(fused, steps, planes, rows, row_width, col_width),
        out_shape=outs,
        in_specs=[pl.BlockSpec(memory_space=pltpu.HBM)] * (1 + len(operands)),
        out_specs=[pl.BlockSpec(memory_space=pltpu.VMEM)] * 4,
        scratch_shapes=scratch,
        compiler_params=pltpu.CompilerParams(
            collective_id=0, has_side_effects=True, vmem_limit_bytes=60 * 2 ** 20
        ),
    )(slab_index, *operands)
    new_x, new_y, new_z, new_core = pl.pallas_call(
        hand_over,
        out_shape=outs,
        in_specs=[pl.BlockSpec(memory_space=pltpu.VMEM)] * 4,
        out_specs=[pl.BlockSpec(memory_space=pltpu.VMEM)] * 4,
        compiler_params=pltpu.CompilerParams(vmem_limit_bytes=60 * 2 ** 20),
    )(*results)
    return new_x, new_y.T, new_z.T, new_core.reshape(core.shape)


def by_collectives(
    slabs, slab_index, omega_x, omega_y, omega_z, phi_x, phi_y, phi_z, sketch_x, sketch_y, sketch_z, core
):
    planes = slabs.shape[1]
    x_parts = lax.axis_size("gx")
    y_parts = lax.axis_size("gy")
    full_size = phi_x.shape[1]
    row_width = full_size // x_parts
    col_width = full_size // y_parts
    for step in range(slabs.shape[0]):
        field = slabs[step]
        first = slab_index[step] * DZ
        start = first + lax.axis_index("wa") * planes
        depth_omega = lax.dynamic_slice_in_dim(omega_z, start, planes, 0)
        depth_phi = lax.dynamic_slice_in_dim(phi_z, start, planes, 0)
        row_mix = contract("zij,jr->zir", field, omega_y)
        rows_part = contract("zir,zr->ir", row_mix, depth_omega)
        plane_part = contract("zir,ir->zr", row_mix, omega_x)
        col_mix = contract("zij,ir->zjr", field, omega_x)
        cols_part = contract("zjr,zr->jr", col_mix, depth_omega)
        core_cols = contract("zij,jb->zib", field, phi_y)
        sketch_x = sketch_x + lax.psum(rows_part, ("gy", "wa"))
        sketch_y = sketch_y + lax.psum(cols_part, ("gx", "wa"))
        plane_total = lax.psum(plane_part, ("gx", "gy"))
        slab_rows = lax.all_gather(plane_total, "wa", axis=0, tiled=True)
        current = lax.dynamic_slice_in_dim(sketch_z, first, DZ, 0)
        sketch_z = lax.dynamic_update_slice_in_dim(sketch_z, current + slab_rows, first, 0)
        core_both = contract("zib,ia->zab", core_cols, phi_x)
        blocks = core_both.reshape(planes, x_parts, row_width, y_parts, col_width)
        blocks = blocks.transpose(1, 3, 0, 2, 4).reshape(
            x_parts * y_parts * planes, row_width, col_width
        )
        owned = lax.psum_scatter(blocks, ("gx", "gy"), scatter_dimension=0, tiled=True)
        depth_term = contract("zab,zc->cab", owned, depth_phi)
        core = core + lax.psum_scatter(depth_term, "wa", scatter_dimension=0, tiled=True)
    return (sketch_x, sketch_y, sketch_z, core)


def solution(mesh):
    shape = dict(mesh.shape)
    in_kernel = (shape["gx"], shape["gy"], shape["wa"]) == (4, 2, 2)
    placed = (
        P("runs", "wa", "gx", "gy"),
        P("runs"),
        P("gx", None),
        P("gy", None),
        P(),
        P("gx", None),
        P("gy", None),
        P(),
        P(("runs", "gx"), None),
        P(("runs", "gy"), None),
        P("runs", None),
        P(("runs", "wa"), "gx", "gy"),
    )
    return jax.shard_map(
        one_kernel if in_kernel else by_collectives,
        mesh=mesh,
        in_specs=placed,
        out_specs=(
            P(("runs", "gx"), None),
            P(("runs", "gy"), None),
            P("runs", None),
            P(("runs", "wa"), "gx", "gy"),
        ),
        check_vma=False,
    )
```

```python
import functools

import jax
import jax.numpy as jnp
from jax import lax
from jax.experimental import pallas as pl
from jax.experimental.pallas import tpu as pltpu
from jax.sharding import PartitionSpec as P

DZ = 16
F32 = jnp.float32
BF16 = jnp.bfloat16
LANES = 128
NN = (((1,), (0,)), ((), ()))
NT = (((1,), (1,)), ((), ()))


def contract(form, left, right):
    return jnp.einsum(form, left, right, precision=lax.Precision.HIGHEST)


def split(value):
    high = value.astype(BF16)
    return high, (value - high.astype(F32)).astype(BF16)


def mul(left, right, dims=NN):
    return lax.dot_general(left, right, dims, preferred_element_type=F32)


def mul3(left_high, left_low, right_high, right_low, dims=NN):
    rows = left_high.shape[0]
    both = mul(jnp.concatenate([left_high, left_low], axis=0), right_high, dims)
    return both[:rows] + both[rows:] + mul(left_high, right_low, dims)


def iota(shape, dim):
    return lax.broadcasted_iota(jnp.int32, shape, dim)


def fused(
    steps, planes, rows, row_width, col_width,
    steps_at, slabs, omega_x, omega_y, omega_z, phi_x, phi_y, phi_z, sketch_x, sketch_y, sketch_z, core,
    o_x, o_y, o_z, o_core,
    index, v_slabs, v_ox, v_oy, v_oz, v_px, v_py, v_pz, v_sx, v_sy, v_sz, v_core, in_sem,
    gy_out, gy_in, cols, px_in, raw_in, keep, mid_in, near_in, far_in, total, wa_in,
    mix, parts, row_mix, own_high, own_low, far_high, far_low, y_sum, x_sum, z_sum, hot, depth,
    y_in, xz_out, xz_in, x_out, x_in, rs_out, rs_in, ag_out, ag_all, ag_in, z_out, z_in, z_own, z_far, cube,
    send_sem, recv_sem,
):
    gx, gy, wa = lax.axis_index("gx"), lax.axis_index("gy"), lax.axis_index("wa")
    pair = gx + 1 - 2 * lax.rem(gx, 2)
    across = 3 - gx
    beyond = 3 - pair
    inner = jnp.logical_or(gx == 1, gx == 2)
    outer = jnp.logical_not(inner)
    group = LANES // row_width
    quads = planes // group
    chunks = steps * quads
    size = group * rows
    flat = planes * rows
    full = v_px.shape[1]
    rank = v_oy.shape[0]
    half, fold = rank // 2, rank // 4
    n_sems = [0]

    def local(src, dst, sem):
        return pltpu.make_async_copy(src, dst, sem)

    sources = (phi_y, omega_y, omega_z, omega_x, phi_x, phi_z, sketch_x, sketch_y, sketch_z, core)
    places = (v_py, v_oy, v_oz, v_ox, v_px, v_pz, v_sx, v_sy, v_sz, v_core)
    loads = [local(s, d, in_sem.at[k]) for k, (s, d) in enumerate(zip(sources, places))]
    index_load = local(steps_at, index, in_sem.at[len(loads)])
    fields = []
    for c in range(chunks):
        part = (c // quads, pl.ds(c % quads * size, size))
        fields.append(local(slabs.at[part], v_slabs.at[part], in_sem.at[len(loads) + 1 + c]))
    for copy in loads[:2] + fields[:2] + [index_load] + loads[2:6] + fields[2:] + loads[6:]:
        copy.start()

    barrier = pltpu.get_barrier_semaphore()
    peers = [{"wa": 1 - wa}, {"gy": 1 - gy}, {"gx": pair}, {"gx": across}, {"gx": beyond}]
    for where in peers:
        pl.semaphore_signal(barrier, inc=1, device_id=where, device_id_type=pl.DeviceIdType.MESH)

    def remote(src, dst, where):
        k = n_sems[0]
        n_sems[0] += 1
        return pltpu.make_async_remote_copy(
            src_ref=src, dst_ref=dst, send_sem=send_sem.at[k], recv_sem=recv_sem.at[k],
            device_id=where, device_id_type=pl.DeviceIdType.MESH,
        )

    every = range(chunks)

    def block(c, k):
        return keep.at[c, :, pl.ds(k * LANES, LANES)]

    to_gy = [remote(gy_out.at[c], gy_in.at[c], {"gy": 1 - gy}) for c in every]
    to_px = remote(v_px, px_in, {"gx": pair})
    to_raw = [remote(cols.at[c], raw_in.at[c], {"gx": pair}) for c in every]
    to_near = [remote(block(c, 1), near_in.at[c], {"gx": pair}) for c in every]
    to_mid = [remote(block(c, 2), mid_in.at[c], {"gx": across}) for c in every]
    to_far = [remote(block(c, 3), far_in.at[c], {"gx": beyond}) for c in every]
    to_wa = [remote(total.at[c], wa_in.at[c], {"wa": 1 - wa}) for c in every]
    y_other = pl.ds(pl.multiple_of((1 - wa) * half, half), half)
    y_own = pl.ds(pl.multiple_of(wa * half, half), half)
    to_y = remote(y_sum.at[y_other], y_in, {"wa": 1 - wa})
    to_xz = remote(xz_out, xz_in, {"gy": 1 - gy})
    to_x = remote(x_out, x_in, {"wa": 1 - wa})
    others = (pair, across, beyond)
    to_rs = [remote(rs_out.at[o], rs_in.at[k], {"gx": o}) for k, o in enumerate(others)]
    to_ag = [remote(ag_out, ag_all.at[gx], {"gx": o}) for o in others]
    to_all = remote(ag_all, ag_in, {"wa": 1 - wa})
    to_z = [remote(z_out, z_in.at[k], {"gx": o}) for k, o in enumerate(others)]
    to_zw = remote(z_own, z_far, {"wa": 1 - wa})

    loads[0].wait()
    loads[1].wait()
    for k, part in enumerate(split(jnp.concatenate([v_py[...].T, v_oy[...]], axis=0))):
        mix[k] = part

    held = max(chunks - 2, 1)

    def stage_a(c):
        fields[c].wait()
        part = (c // quads, pl.ds(c % quads * size, size))
        x_high, x_low = split(v_slabs[part])
        parts[0, c * size:(c + 1) * size, :] = x_high
        parts[1, c * size:(c + 1) * size, :] = x_low
        mixed = mul3(mix[0], mix[1], x_high, x_low, NT)
        for k in range(2):
            @pl.when(gy == k)
            def _():
                cols[c] = mixed[k * col_width:(k + 1) * col_width]
                gy_out[c] = mixed[(1 - k) * col_width:(2 - k) * col_width]
        row_mix[:, c * size:(c + 1) * size] = mixed[full:]
        if c == 0:
            pl.semaphore_wait(barrier, len(peers))

            @pl.when(outer)
            def _():
                loads[4].wait()
                to_px.start()
        if c < held:
            to_gy[c].start()

    depth_count = steps * planes

    def rows_of(offsets):
        lane = iota((v_oz.shape[1], LANES), 1)
        wanted = jnp.full(lane.shape, -1, jnp.int32)
        for k, offset in enumerate(offsets):
            for t in range(steps):
                first = k * depth_count + t * planes
                inside = jnp.logical_and(lane >= first, lane < first + planes)
                wanted = jnp.where(inside, lane - first + (index[t] * DZ + offset), wanted)
        return (iota(lane.shape, 0) == wanted).astype(BF16)

    def sketches(t, oz_high, oz_low, ox_tiles):
        shape = (LANES, flat)
        spread = (iota(shape, 0) == t * planes + iota(shape, 1) // rows).astype(BF16)
        weight = mul(oz_high, spread) + mul(oz_low, spread)
        w_high, w_low = split(weight * ox_tiles)
        here = pl.ds(t * flat, flat)
        y_part = mul3(w_high, w_low, parts[0, here, :], parts[1, here, :])
        mixed = row_mix[:, here]
        weighted = mixed * weight
        x_part = functools.reduce(jnp.add, [weighted[:, k:k + LANES] for k in range(0, flat, LANES)])
        m_high, m_low = split(mixed * ox_tiles)
        z_part = mul(m_high, spread, NT) + mul(m_low, spread, NT)
        for ref, part in ((y_sum, y_part), (x_sum, x_part), (z_sum, z_part)):
            ref[...] = part if t == 0 else ref[...] + part

    def blocks_of(phi, high_ref, low_ref):
        phi_high, phi_low = split(phi)
        k, l = iota((full, LANES), 0), iota((full, LANES), 1)
        same = iota((size, LANES), 0) // rows == iota((size, LANES), 1) // row_width
        for o, owner in enumerate((gx, pair, across, beyond)):
            chosen = (k == owner * row_width + lax.rem(l, row_width)).astype(BF16)
            for part, ref in ((phi_high, high_ref), (phi_low, low_ref)):
                tiled = jnp.concatenate([mul(part, chosen)] * group, axis=0)
                ref[:, o * LANES:(o + 1) * LANES] = jnp.where(same, tiled, 0.0).astype(BF16)

    def stage_b(c):
        to_gy[c].wait_recv()
        cols[c] = cols[c] + gy_in[c]

        @pl.when(outer)
        def _():
            to_raw[c].start()

        @pl.when(inner)
        def _():
            high, low = split(cols[c])
            keep[c] = mul3(high, low, own_high[...], own_low[...])

    def stage_c(c):
        @pl.when(inner)
        def _():
            to_raw[c].wait_recv()
            high, low = split(raw_in[c])
            keep[c] = keep[c] + mul3(high, low, far_high[...], far_low[...])
            to_far[c].start()
            to_mid[c].start()
            to_near[c].start()

    def stage_d(c):
        @pl.when(inner)
        def _():
            to_mid[c].wait_recv()
            total[c] = keep[c, :, :LANES] + mid_in[c]

        @pl.when(outer)
        def _():
            to_near[c].wait_recv()
            to_far[c].wait_recv()
            total[c] = near_in[c] + far_in[c]

        to_wa[c].start()
        turn(0, c, total)

    def turn(which, c, ref):
        first = (which * chunks + c) * LANES
        cube[first:first + LANES, :] = ref[c].T

    def stage_f(c):
        to_wa[c].wait_recv()
        turn(1, c, wa_in)

    def moved(value, start):
        shape = (LANES, LANES)
        back, ahead = (0, start) if start >= 0 else (-start, 0)
        source, place = iota(shape, 0) - back, iota(shape, 1) - ahead
        same = jnp.logical_and(source == place, jnp.logical_and(source >= 0, source < LANES // 4))
        high, low = split(value)
        return mul(high, same.astype(BF16)) + mul(low, same.astype(BF16))

    def sums_1():
        to_y.start()
        xz_out[:rank, :] = x_sum[...]
        xz_out[rank:, :] = functools.reduce(
            jnp.add, [moved(z_sum[k * fold:(k + 1) * fold, :], k * LANES // 4) for k in range(4)]
        )
        to_xz.start()
        for c in range(held, chunks):
            to_gy[c].start()

    def sums_y1():
        to_y.wait_recv()
        y_half = y_sum[y_own, :] + y_in[...]
        for k in range(4):
            rs_out[k] = y_half[:, k * LANES:(k + 1) * LANES]
        for copy in to_rs:
            copy.start()

    def sums_xz():
        to_xz.wait_recv()
        both = xz_out[...] + xz_in[...]
        z_out[...] = both[rank:]
        for copy in to_z:
            copy.start()
        x_out[...] = both[:rank]
        to_x.start()

    def sums_y2():
        for copy in to_rs:
            copy.wait_recv()
        summed = rs_out[gx] + rs_in[0] + rs_in[1] + rs_in[2]
        ag_out[...] = summed
        for copy in to_ag:
            copy.start()
        ag_all[gx] = summed

    def sums_z():
        for copy in to_z:
            copy.wait_recv()
        z_own[...] = z_out[...] + z_in[0] + z_in[1] + z_in[2]
        to_zw.start()
        to_x.wait_recv()
        x_all = x_out[...] + x_in[...]
        loads[6].wait()
        o_x[...] = v_sx[...] + (x_all[:, :rows] + x_all[:, rows:]).T

    def sums_y3():
        for copy in to_ag:
            copy.wait_recv()
        to_all.start()

    def sums_last():
        to_zw.wait_recv()
        loads[8].wait()
        value = v_sz[...]
        for ref, places in ((z_own, hot[0]), (z_far, hot[1])):
            whole = jnp.concatenate([moved(ref[...], -(k * LANES // 4)) for k in range(4)], axis=0)
            for part in split(whole):
                value = value + mul(part, places, NT)
        o_z[...] = value
        to_all.wait_recv()
        loads[7].wait()
        for k in range(4):
            lanes = slice(k * LANES, (k + 1) * LANES)
            o_y[y_own, lanes] = v_sy[y_own, lanes] + ag_all[k]
            o_y[y_other, lanes] = v_sy[y_other, lanes] + ag_in[k]

    stage_a(0)
    stage_a(1)
    index_load.wait()
    for k in (2, 3, 5):
        loads[k].wait()
    hot[0] = rows_of((wa * planes, (1 - wa) * planes))
    hot[1] = rows_of(((1 - wa) * planes,))
    oz_high, oz_low = (mul(part, hot[0]).astype(BF16) for part in split(v_oz[...]))
    ox_tiles = jnp.concatenate([v_ox[...].T] * planes, axis=1)
    for c in range(2, chunks):
        stage_a(c)

    @pl.when(inner)
    def _():
        loads[4].wait()
        blocks_of(v_px[...], own_high, own_low)
        to_px.wait_recv()
        blocks_of(px_in[...], far_high, far_low)

    for t in range(steps):
        sketches(t, oz_high, oz_low, ox_tiles)
        if t < steps - 1:
            stage_b(t)
    sums_1()
    for k, part in enumerate(split(v_pz[...])):
        depth[k] = mul(part, hot[0])

    between = {1: sums_y1, 2: sums_xz, 3: sums_y2, 4: sums_z, 5: sums_y3, 6: sums_last}
    first = steps - 1
    for s in range(chunks + 4):
        if first + s < chunks:
            stage_b(first + s)
        if s < chunks:
            stage_c(s)
        if s in between:
            between[s]()
        if 0 <= s - 2 < chunks:
            stage_d(s - 2)
        if 0 <= s - 3 < chunks:
            stage_f(s - 3)

    loads[9].wait()
    owned = v_pz.shape[0] // 2
    count = 2 * depth_count
    spot = pl.ds(pl.multiple_of(wa * owned, owned), owned)
    p_high, p_low = (depth[k, spot, :][:, :count].astype(BF16) for k in range(2))
    for a in range(row_width):
        high, low = split(cube[pl.ds(a, count, stride=row_width), :])
        spot = pl.ds(a, owned, stride=row_width)
        o_core[spot, :] = v_core[spot, :] + mul3(p_high, p_low, high, low)

    for copy in to_gy + to_wa + [to_y, to_xz, to_x, to_all, to_zw] + to_rs + to_ag + to_z:
        copy.wait_send()

    @pl.when(outer)
    def _():
        for copy in to_raw + [to_px]:
            copy.wait_send()

    @pl.when(inner)
    def _():
        for copy in to_near + to_mid + to_far:
            copy.wait_send()


def hand_over(*refs):
    for source, place in zip(refs[:4], refs[4:]):
        place[...] = source[...]


def one_kernel(
    slabs, slab_index, omega_x, omega_y, omega_z, phi_x, phi_y, phi_z, sketch_x, sketch_y, sketch_z, core
):
    steps, planes, rows, width = slabs.shape
    rank, full = omega_x.shape[1], phi_x.shape[1]
    row_width, col_width = core.shape[1], core.shape[2]
    group = LANES // row_width
    chunks = steps * planes // group
    size = group * rows
    half, fold = rank // 2, rank // 4
    vmem = lambda shape, kind=F32: pltpu.VMEM(shape, kind)
    like = lambda value: vmem(value.shape)
    flat_core = core.reshape(-1, col_width)
    operands = (
        slabs.reshape(steps, planes * rows, width), omega_x, omega_y.T, omega_z.T, phi_x, phi_y, phi_z.T,
        sketch_x, sketch_y.T, sketch_z.T, flat_core,
    )
    scratch = [pltpu.SMEM(slab_index.shape, jnp.int32)] + [like(value) for value in operands]
    scratch += [
        pltpu.SemaphoreType.DMA((11 + chunks,)),
        *(vmem((chunks, col_width, size)) for _ in range(3)),
        vmem((rows, full)), vmem((chunks, col_width, size)),
        vmem((chunks, col_width, 4 * LANES)),
        *(vmem((chunks, col_width, LANES)) for _ in range(5)),
        vmem((2, full + rank, width), BF16), vmem((2, chunks * size, width), BF16), vmem((rank, chunks * size)),
        *(vmem((size, 4 * LANES), BF16) for _ in range(4)),
        vmem((rank, width)), vmem((rank, LANES)), vmem((rank, LANES)),
        vmem((2, omega_z.shape[0], LANES), BF16), vmem((2, phi_z.shape[1], LANES)),
        vmem((half, width)), vmem((rank + fold, LANES)), vmem((rank + fold, LANES)),
        vmem((rank, LANES)), vmem((rank, LANES)),
        vmem((4, half, LANES)), vmem((3, half, LANES)), vmem((half, LANES)),
        vmem((4, half, LANES)), vmem((4, half, LANES)),
        vmem((fold, LANES)), vmem((3, fold, LANES)), vmem((fold, LANES)), vmem((fold, LANES)),
        vmem((2 * steps * planes * row_width, col_width)),
        pltpu.SemaphoreType.DMA((7 * chunks + 15,)),
        pltpu.SemaphoreType.DMA((7 * chunks + 15,)),
    ]
    outs = [jax.ShapeDtypeStruct(v.shape, F32) for v in operands[-4:]]
    results = pl.pallas_call(
        functools.partial(fused, steps, planes, rows, row_width, col_width),
        out_shape=outs,
        in_specs=[pl.BlockSpec(memory_space=pltpu.HBM)] * (1 + len(operands)),
        out_specs=[pl.BlockSpec(memory_space=pltpu.VMEM)] * 4,
        scratch_shapes=scratch,
        compiler_params=pltpu.CompilerParams(
            collective_id=0, has_side_effects=True, vmem_limit_bytes=60 * 2 ** 20
        ),
    )(slab_index, *operands)
    new_x, new_y, new_z, new_core = pl.pallas_call(
        hand_over,
        out_shape=outs,
        in_specs=[pl.BlockSpec(memory_space=pltpu.VMEM)] * 4,
        out_specs=[pl.BlockSpec(memory_space=pltpu.VMEM)] * 4,
        compiler_params=pltpu.CompilerParams(vmem_limit_bytes=60 * 2 ** 20),
    )(*results)
    return new_x, new_y.T, new_z.T, new_core.reshape(core.shape)


def by_collectives(
    slabs, slab_index, omega_x, omega_y, omega_z, phi_x, phi_y, phi_z, sketch_x, sketch_y, sketch_z, core
):
    planes = slabs.shape[1]
    x_parts = lax.axis_size("gx")
    y_parts = lax.axis_size("gy")
    full_size = phi_x.shape[1]
    row_width = full_size // x_parts
    col_width = full_size // y_parts
    for step in range(slabs.shape[0]):
        field = slabs[step]
        first = slab_index[step] * DZ
        start = first + lax.axis_index("wa") * planes
        depth_omega = lax.dynamic_slice_in_dim(omega_z, start, planes, 0)
        depth_phi = lax.dynamic_slice_in_dim(phi_z, start, planes, 0)
        row_mix = contract("zij,jr->zir", field, omega_y)
        rows_part = contract("zir,zr->ir", row_mix, depth_omega)
        plane_part = contract("zir,ir->zr", row_mix, omega_x)
        col_mix = contract("zij,ir->zjr", field, omega_x)
        cols_part = contract("zjr,zr->jr", col_mix, depth_omega)
        core_cols = contract("zij,jb->zib", field, phi_y)
        sketch_x = sketch_x + lax.psum(rows_part, ("gy", "wa"))
        sketch_y = sketch_y + lax.psum(cols_part, ("gx", "wa"))
        plane_total = lax.psum(plane_part, ("gx", "gy"))
        slab_rows = lax.all_gather(plane_total, "wa", axis=0, tiled=True)
        current = lax.dynamic_slice_in_dim(sketch_z, first, DZ, 0)
        sketch_z = lax.dynamic_update_slice_in_dim(sketch_z, current + slab_rows, first, 0)
        core_both = contract("zib,ia->zab", core_cols, phi_x)
        blocks = core_both.reshape(planes, x_parts, row_width, y_parts, col_width)
        blocks = blocks.transpose(1, 3, 0, 2, 4).reshape(
            x_parts * y_parts * planes, row_width, col_width
        )
        owned = lax.psum_scatter(blocks, ("gx", "gy"), scatter_dimension=0, tiled=True)
        depth_term = contract("zab,zc->cab", owned, depth_phi)
        core = core + lax.psum_scatter(depth_term, "wa", scatter_dimension=0, tiled=True)
    return (sketch_x, sketch_y, sketch_z, core)


def solution(mesh):
    shape = dict(mesh.shape)
    in_kernel = (shape["gx"], shape["gy"], shape["wa"]) == (4, 2, 2)
    placed = (
        P("runs", "wa", "gx", "gy"),
        P("runs"),
        P("gx", None),
        P("gy", None),
        P(),
        P("gx", None),
        P("gy", None),
        P(),
        P(("runs", "gx"), None),
        P(("runs", "gy"), None),
        P("runs", None),
        P(("runs", "wa"), "gx", "gy"),
    )
    return jax.shard_map(
        one_kernel if in_kernel else by_collectives,
        mesh=mesh,
        in_specs=placed,
        out_specs=(
            P(("runs", "gx"), None),
            P(("runs", "gy"), None),
            P("runs", None),
            P(("runs", "wa"), "gx", "gy"),
        ),
        check_vma=False,
    )
```

```python
import functools

import jax
import jax.numpy as jnp
from jax import lax
from jax.experimental import pallas as pl
from jax.experimental.pallas import tpu as pltpu
from jax.sharding import PartitionSpec as P

DZ = 16
F32 = jnp.float32
BF16 = jnp.bfloat16
LANES = 128
NN = (((1,), (0,)), ((), ()))
NT = (((1,), (1,)), ((), ()))


def contract(form, left, right):
    return jnp.einsum(form, left, right, precision=lax.Precision.HIGHEST)


def split(value):
    high = value.astype(BF16)
    return high, (value - high.astype(F32)).astype(BF16)


def mul(left, right, dims=NN):
    return lax.dot_general(left, right, dims, preferred_element_type=F32)


def mul3(left_high, left_low, right_high, right_low, dims=NN):
    rows = left_high.shape[0]
    both = mul(jnp.concatenate([left_high, left_low], axis=0), right_high, dims)
    return both[:rows] + both[rows:] + mul(left_high, right_low, dims)


def iota(shape, dim):
    return lax.broadcasted_iota(jnp.int32, shape, dim)


def fused(
    steps, planes, rows, row_width, col_width,
    steps_at, slabs, omega_x, omega_y, omega_z, phi_x, phi_y, phi_z, sketch_x, sketch_y, sketch_z, core,
    o_x, o_y, o_z, o_core,
    index, v_slabs, v_ox, v_oy, v_oz, v_px, v_py, v_pz, v_sx, v_sy, v_sz, v_core, in_sem,
    gy_out, gy_in, cols, px_in, raw_in, keep, mid_in, near_in, far_in, total, wa_in,
    mix, parts, row_mix, own_high, own_low, far_high, far_low, y_sum, x_sum, z_sum, hot, depth,
    y_in, xz_out, xz_in, x_out, x_in, rs_out, rs_in, ag_out, ag_all, ag_in, z_out, z_in, z_own, z_far, cube,
    send_sem, recv_sem,
):
    gx, gy, wa = lax.axis_index("gx"), lax.axis_index("gy"), lax.axis_index("wa")
    pair = gx + 1 - 2 * lax.rem(gx, 2)
    across = 3 - gx
    beyond = 3 - pair
    inner = jnp.logical_or(gx == 1, gx == 2)
    outer = jnp.logical_not(inner)
    group = LANES // row_width
    quads = planes // group
    chunks = steps * quads
    size = group * rows
    flat = planes * rows
    full = v_px.shape[1]
    rank = v_oy.shape[0]
    half, fold = rank // 2, rank // 4
    n_sems = [0]

    def local(src, dst, sem):
        return pltpu.make_async_copy(src, dst, sem)

    sources = (phi_y, omega_y, omega_z, omega_x, phi_x, phi_z, sketch_x, sketch_y, sketch_z, core)
    places = (v_py, v_oy, v_oz, v_ox, v_px, v_pz, v_sx, v_sy, v_sz, v_core)
    loads = [local(s, d, in_sem.at[k]) for k, (s, d) in enumerate(zip(sources, places))]
    index_load = local(steps_at, index, in_sem.at[len(loads)])
    fields = []
    for c in range(chunks):
        part = (c // quads, pl.ds(c % quads * size, size))
        fields.append(local(slabs.at[part], v_slabs.at[part], in_sem.at[len(loads) + 1 + c]))
    for copy in loads[:2] + fields[:2] + [index_load] + loads[2:6] + fields[2:] + loads[6:]:
        copy.start()

    barrier = pltpu.get_barrier_semaphore()
    peers = [{"wa": 1 - wa}, {"gy": 1 - gy}, {"gx": pair}, {"gx": across}, {"gx": beyond}]
    for where in peers:
        pl.semaphore_signal(barrier, inc=1, device_id=where, device_id_type=pl.DeviceIdType.MESH)

    def remote(src, dst, where):
        k = n_sems[0]
        n_sems[0] += 1
        return pltpu.make_async_remote_copy(
            src_ref=src, dst_ref=dst, send_sem=send_sem.at[k], recv_sem=recv_sem.at[k],
            device_id=where, device_id_type=pl.DeviceIdType.MESH,
        )

    every = range(chunks)

    def block(c, k):
        return keep.at[c, :, pl.ds(k * LANES, LANES)]

    to_gy = [remote(gy_out.at[c], gy_in.at[c], {"gy": 1 - gy}) for c in every]
    to_px = remote(v_px, px_in, {"gx": pair})
    to_raw = [remote(cols.at[c], raw_in.at[c], {"gx": pair}) for c in every]
    to_near = [remote(block(c, 1), near_in.at[c], {"gx": pair}) for c in every]
    to_mid = [remote(block(c, 2), mid_in.at[c], {"gx": across}) for c in every]
    to_far = [remote(block(c, 3), far_in.at[c], {"gx": beyond}) for c in every]
    to_wa = [remote(total.at[c], wa_in.at[c], {"wa": 1 - wa}) for c in every]
    y_other = pl.ds(pl.multiple_of((1 - wa) * half, half), half)
    y_own = pl.ds(pl.multiple_of(wa * half, half), half)
    to_y = remote(y_sum.at[y_other], y_in, {"wa": 1 - wa})
    to_xz = remote(xz_out, xz_in, {"gy": 1 - gy})
    to_x = remote(x_out, x_in, {"wa": 1 - wa})
    others = (pair, across, beyond)
    to_rs = [remote(rs_out.at[o], rs_in.at[k], {"gx": o}) for k, o in enumerate(others)]
    to_ag = [remote(ag_out, ag_all.at[gx], {"gx": o}) for o in others]
    to_all = remote(ag_all, ag_in, {"wa": 1 - wa})
    to_z = [remote(z_out, z_in.at[k], {"gx": o}) for k, o in enumerate(others)]
    to_zw = remote(z_own, z_far, {"wa": 1 - wa})

    loads[0].wait()
    loads[1].wait()
    for k, part in enumerate(split(jnp.concatenate([v_py[...].T, v_oy[...]], axis=0))):
        mix[k] = part

    held = max(chunks - 2, 1)

    def stage_a(c):
        fields[c].wait()
        part = (c // quads, pl.ds(c % quads * size, size))
        x_high, x_low = split(v_slabs[part])
        parts[0, c * size:(c + 1) * size, :] = x_high
        parts[1, c * size:(c + 1) * size, :] = x_low
        mixed = mul3(mix[0], mix[1], x_high, x_low, NT)
        for k in range(2):
            @pl.when(gy == k)
            def _():
                cols[c] = mixed[k * col_width:(k + 1) * col_width]
                gy_out[c] = mixed[(1 - k) * col_width:(2 - k) * col_width]
        row_mix[:, c * size:(c + 1) * size] = mixed[full:]
        if c == 0:
            pl.semaphore_wait(barrier, len(peers))

            @pl.when(outer)
            def _():
                loads[4].wait()
                to_px.start()
        if c < held:
            to_gy[c].start()

    depth_count = steps * planes

    def rows_of(offsets):
        lane = iota((v_oz.shape[1], LANES), 1)
        wanted = jnp.full(lane.shape, -1, jnp.int32)
        for k, offset in enumerate(offsets):
            for t in range(steps):
                first = k * depth_count + t * planes
                inside = jnp.logical_and(lane >= first, lane < first + planes)
                wanted = jnp.where(inside, lane - first + (index[t] * DZ + offset), wanted)
        return (iota(lane.shape, 0) == wanted).astype(BF16)

    def sketches(t, oz_high, oz_low, ox_tiles):
        shape = (LANES, flat)
        spread = (iota(shape, 0) == t * planes + iota(shape, 1) // rows).astype(BF16)
        weight = mul(oz_high, spread) + mul(oz_low, spread)
        w_high, w_low = split(weight * ox_tiles)
        here = pl.ds(t * flat, flat)
        y_part = mul3(w_high, w_low, parts[0, here, :], parts[1, here, :])
        mixed = row_mix[:, here]
        weighted = mixed * weight
        x_part = functools.reduce(jnp.add, [weighted[:, k:k + LANES] for k in range(0, flat, LANES)])
        m_high, m_low = split(mixed * ox_tiles)
        z_part = mul(m_high, spread, NT) + mul(m_low, spread, NT)
        for ref, part in ((y_sum, y_part), (x_sum, x_part), (z_sum, z_part)):
            ref[...] = part if t == 0 else ref[...] + part

    def blocks_of(phi, high_ref, low_ref):
        phi_high, phi_low = split(phi)
        k, l = iota((full, LANES), 0), iota((full, LANES), 1)
        same = iota((size, LANES), 0) // rows == iota((size, LANES), 1) // row_width
        for o, owner in enumerate((gx, pair, across, beyond)):
            chosen = (k == owner * row_width + lax.rem(l, row_width)).astype(BF16)
            for part, ref in ((phi_high, high_ref), (phi_low, low_ref)):
                tiled = jnp.concatenate([mul(part, chosen)] * group, axis=0)
                ref[:, o * LANES:(o + 1) * LANES] = jnp.where(same, tiled, 0.0).astype(BF16)

    def stage_b(c):
        to_gy[c].wait_recv()
        cols[c] = cols[c] + gy_in[c]

        @pl.when(outer)
        def _():
            to_raw[c].start()

        @pl.when(inner)
        def _():
            high, low = split(cols[c])
            keep[c] = mul3(high, low, own_high[...], own_low[...])

    def stage_c(c):
        @pl.when(inner)
        def _():
            to_raw[c].wait_recv()
            high, low = split(raw_in[c])
            keep[c] = keep[c] + mul3(high, low, far_high[...], far_low[...])
            to_far[c].start()
            to_mid[c].start()
            to_near[c].start()

    def stage_d(c):
        @pl.when(inner)
        def _():
            to_mid[c].wait_recv()
            total[c] = keep[c, :, :LANES] + mid_in[c]

        @pl.when(outer)
        def _():
            to_near[c].wait_recv()
            to_far[c].wait_recv()
            total[c] = near_in[c] + far_in[c]

        to_wa[c].start()
        turn(0, c, total)

    def turn(which, c, ref):
        first = (which * chunks + c) * LANES
        cube[first:first + LANES, :] = ref[c].T

    def stage_f(c):
        to_wa[c].wait_recv()
        turn(1, c, wa_in)

    def moved(value, start):
        shape = (LANES, LANES)
        back, ahead = (0, start) if start >= 0 else (-start, 0)
        source, place = iota(shape, 0) - back, iota(shape, 1) - ahead
        same = jnp.logical_and(source == place, jnp.logical_and(source >= 0, source < LANES // 4))
        high, low = split(value)
        return mul(high, same.astype(BF16)) + mul(low, same.astype(BF16))

    def sums_1():
        to_y.start()
        xz_out[:rank, :] = x_sum[...]
        xz_out[rank:, :] = functools.reduce(
            jnp.add, [moved(z_sum[k * fold:(k + 1) * fold, :], k * LANES // 4) for k in range(4)]
        )
        to_xz.start()
        for c in range(held, chunks):
            to_gy[c].start()

    def sums_y1():
        to_y.wait_recv()
        y_half = y_sum[y_own, :] + y_in[...]
        for k in range(4):
            rs_out[k] = y_half[:, k * LANES:(k + 1) * LANES]
        for copy in to_rs:
            copy.start()

    def sums_xz():
        to_xz.wait_recv()
        both = xz_out[...] + xz_in[...]
        z_out[...] = both[rank:]
        for copy in to_z:
            copy.start()
        x_out[...] = both[:rank]
        to_x.start()

    def sums_y2():
        for copy in to_rs:
            copy.wait_recv()
        summed = rs_out[gx] + rs_in[0] + rs_in[1] + rs_in[2]
        ag_out[...] = summed
        for copy in to_ag:
            copy.start()
        ag_all[gx] = summed

    def sums_z():
        for copy in to_z:
            copy.wait_recv()
        z_own[...] = z_out[...] + z_in[0] + z_in[1] + z_in[2]
        to_zw.start()
        to_x.wait_recv()
        x_all = x_out[...] + x_in[...]
        loads[6].wait()
        o_x[...] = v_sx[...] + (x_all[:, :rows] + x_all[:, rows:]).T

    def sums_y3():
        for copy in to_ag:
            copy.wait_recv()
        to_all.start()

    def sums_last():
        to_zw.wait_recv()
        loads[8].wait()
        value = v_sz[...]
        for ref, places in ((z_own, hot[0]), (z_far, hot[1])):
            whole = jnp.concatenate([moved(ref[...], -(k * LANES // 4)) for k in range(4)], axis=0)
            for part in split(whole):
                value = value + mul(part, places, NT)
        o_z[...] = value
        to_all.wait_recv()
        loads[7].wait()
        for k in range(4):
            lanes = slice(k * LANES, (k + 1) * LANES)
            o_y[y_own, lanes] = v_sy[y_own, lanes] + ag_all[k]
            o_y[y_other, lanes] = v_sy[y_other, lanes] + ag_in[k]

    stage_a(0)
    stage_a(1)
    index_load.wait()
    for k in (2, 3, 5):
        loads[k].wait()
    hot[0] = rows_of((wa * planes, (1 - wa) * planes))
    hot[1] = rows_of(((1 - wa) * planes,))
    oz_high, oz_low = (mul(part, hot[0]).astype(BF16) for part in split(v_oz[...]))
    ox_tiles = jnp.concatenate([v_ox[...].T] * planes, axis=1)
    for c in range(2, chunks):
        stage_a(c)

    @pl.when(inner)
    def _():
        loads[4].wait()
        blocks_of(v_px[...], own_high, own_low)
        to_px.wait_recv()
        blocks_of(px_in[...], far_high, far_low)

    for t in range(steps):
        sketches(t, oz_high, oz_low, ox_tiles)
        if t < steps - 1:
            stage_b(t)
    sums_1()
    for k, part in enumerate(split(v_pz[...])):
        depth[k] = mul(part, hot[0])

    between = {0: sums_y1, 2: sums_xz, 3: sums_y2, 5: sums_z, 6: sums_y3, 8: sums_last}
    first = steps - 1
    for s in range(chunks + 4):
        if first + s < chunks:
            stage_b(first + s)
        if s < chunks:
            stage_c(s)
        if s in between:
            between[s]()
        if 0 <= s - 2 < chunks:
            stage_d(s - 2)
        if 0 <= s - 3 < chunks:
            stage_f(s - 3)

    loads[9].wait()
    owned = v_pz.shape[0] // 2
    count = 2 * depth_count
    spot = pl.ds(pl.multiple_of(wa * owned, owned), owned)
    p_high, p_low = (depth[k, spot, :][:, :count].astype(BF16) for k in range(2))
    for a in range(row_width):
        high, low = split(cube[pl.ds(a, count, stride=row_width), :])
        spot = pl.ds(a, owned, stride=row_width)
        o_core[spot, :] = v_core[spot, :] + mul3(p_high, p_low, high, low)

    for copy in to_gy + to_wa + [to_y, to_xz, to_x, to_all, to_zw] + to_rs + to_ag + to_z:
        copy.wait_send()

    @pl.when(outer)
    def _():
        for copy in to_raw + [to_px]:
            copy.wait_send()

    @pl.when(inner)
    def _():
        for copy in to_near + to_mid + to_far:
            copy.wait_send()


def hand_over(*refs):
    for source, place in zip(refs[:4], refs[4:]):
        place[...] = source[...]


def one_kernel(
    slabs, slab_index, omega_x, omega_y, omega_z, phi_x, phi_y, phi_z, sketch_x, sketch_y, sketch_z, core
):
    steps, planes, rows, width = slabs.shape
    rank, full = omega_x.shape[1], phi_x.shape[1]
    row_width, col_width = core.shape[1], core.shape[2]
    group = LANES // row_width
    chunks = steps * planes // group
    size = group * rows
    half, fold = rank // 2, rank // 4
    vmem = lambda shape, kind=F32: pltpu.VMEM(shape, kind)
    like = lambda value: vmem(value.shape)
    flat_core = core.reshape(-1, col_width)
    operands = (
        slabs.reshape(steps, planes * rows, width), omega_x, omega_y.T, omega_z.T, phi_x, phi_y, phi_z.T,
        sketch_x, sketch_y.T, sketch_z.T, flat_core,
    )
    scratch = [pltpu.SMEM(slab_index.shape, jnp.int32)] + [like(value) for value in operands]
    scratch += [
        pltpu.SemaphoreType.DMA((11 + chunks,)),
        *(vmem((chunks, col_width, size)) for _ in range(3)),
        vmem((rows, full)), vmem((chunks, col_width, size)),
        vmem((chunks, col_width, 4 * LANES)),
        *(vmem((chunks, col_width, LANES)) for _ in range(5)),
        vmem((2, full + rank, width), BF16), vmem((2, chunks * size, width), BF16), vmem((rank, chunks * size)),
        *(vmem((size, 4 * LANES), BF16) for _ in range(4)),
        vmem((rank, width)), vmem((rank, LANES)), vmem((rank, LANES)),
        vmem((2, omega_z.shape[0], LANES), BF16), vmem((2, phi_z.shape[1], LANES)),
        vmem((half, width)), vmem((rank + fold, LANES)), vmem((rank + fold, LANES)),
        vmem((rank, LANES)), vmem((rank, LANES)),
        vmem((4, half, LANES)), vmem((3, half, LANES)), vmem((half, LANES)),
        vmem((4, half, LANES)), vmem((4, half, LANES)),
        vmem((fold, LANES)), vmem((3, fold, LANES)), vmem((fold, LANES)), vmem((fold, LANES)),
        vmem((2 * steps * planes * row_width, col_width)),
        pltpu.SemaphoreType.DMA((7 * chunks + 15,)),
        pltpu.SemaphoreType.DMA((7 * chunks + 15,)),
    ]
    outs = [jax.ShapeDtypeStruct(v.shape, F32) for v in operands[-4:]]
    results = pl.pallas_call(
        functools.partial(fused, steps, planes, rows, row_width, col_width),
        out_shape=outs,
        in_specs=[pl.BlockSpec(memory_space=pltpu.HBM)] * (1 + len(operands)),
        out_specs=[pl.BlockSpec(memory_space=pltpu.VMEM)] * 4,
        scratch_shapes=scratch,
        compiler_params=pltpu.CompilerParams(
            collective_id=0, has_side_effects=True, vmem_limit_bytes=60 * 2 ** 20
        ),
    )(slab_index, *operands)
    new_x, new_y, new_z, new_core = pl.pallas_call(
        hand_over,
        out_shape=outs,
        in_specs=[pl.BlockSpec(memory_space=pltpu.VMEM)] * 4,
        out_specs=[pl.BlockSpec(memory_space=pltpu.VMEM)] * 4,
        compiler_params=pltpu.CompilerParams(vmem_limit_bytes=60 * 2 ** 20),
    )(*results)
    return new_x, new_y.T, new_z.T, new_core.reshape(core.shape)


def by_collectives(
    slabs, slab_index, omega_x, omega_y, omega_z, phi_x, phi_y, phi_z, sketch_x, sketch_y, sketch_z, core
):
    planes = slabs.shape[1]
    x_parts = lax.axis_size("gx")
    y_parts = lax.axis_size("gy")
    full_size = phi_x.shape[1]
    row_width = full_size // x_parts
    col_width = full_size // y_parts
    for step in range(slabs.shape[0]):
        field = slabs[step]
        first = slab_index[step] * DZ
        start = first + lax.axis_index("wa") * planes
        depth_omega = lax.dynamic_slice_in_dim(omega_z, start, planes, 0)
        depth_phi = lax.dynamic_slice_in_dim(phi_z, start, planes, 0)
        row_mix = contract("zij,jr->zir", field, omega_y)
        rows_part = contract("zir,zr->ir", row_mix, depth_omega)
        plane_part = contract("zir,ir->zr", row_mix, omega_x)
        col_mix = contract("zij,ir->zjr", field, omega_x)
        cols_part = contract("zjr,zr->jr", col_mix, depth_omega)
        core_cols = contract("zij,jb->zib", field, phi_y)
        sketch_x = sketch_x + lax.psum(rows_part, ("gy", "wa"))
        sketch_y = sketch_y + lax.psum(cols_part, ("gx", "wa"))
        plane_total = lax.psum(plane_part, ("gx", "gy"))
        slab_rows = lax.all_gather(plane_total, "wa", axis=0, tiled=True)
        current = lax.dynamic_slice_in_dim(sketch_z, first, DZ, 0)
        sketch_z = lax.dynamic_update_slice_in_dim(sketch_z, current + slab_rows, first, 0)
        core_both = contract("zib,ia->zab", core_cols, phi_x)
        blocks = core_both.reshape(planes, x_parts, row_width, y_parts, col_width)
        blocks = blocks.transpose(1, 3, 0, 2, 4).reshape(
            x_parts * y_parts * planes, row_width, col_width
        )
        owned = lax.psum_scatter(blocks, ("gx", "gy"), scatter_dimension=0, tiled=True)
        depth_term = contract("zab,zc->cab", owned, depth_phi)
        core = core + lax.psum_scatter(depth_term, "wa", scatter_dimension=0, tiled=True)
    return (sketch_x, sketch_y, sketch_z, core)


def solution(mesh):
    shape = dict(mesh.shape)
    in_kernel = (shape["gx"], shape["gy"], shape["wa"]) == (4, 2, 2)
    placed = (
        P("runs", "wa", "gx", "gy"),
        P("runs"),
        P("gx", None),
        P("gy", None),
        P(),
        P("gx", None),
        P("gy", None),
        P(),
        P(("runs", "gx"), None),
        P(("runs", "gy"), None),
        P("runs", None),
        P(("runs", "wa"), "gx", "gy"),
    )
    return jax.shard_map(
        one_kernel if in_kernel else by_collectives,
        mesh=mesh,
        in_specs=placed,
        out_specs=(
            P(("runs", "gx"), None),
            P(("runs", "gy"), None),
            P("runs", None),
            P(("runs", "wa"), "gx", "gy"),
        ),
        check_vma=False,
    )
```
